256 devices in a mesh: row: 8 (over x, core), col: 16 (over y_lo, z), layer: 2 (over y_hi).
Axes of the slice: x: 4, y: 4 (y_hi: 2, y_lo: 2; y = y_hi * 2 + y_lo), z: 8, core: 2. Of those that a mesh axis runs over, the one named last changes fastest.
Arguments:
- a_vals: bfloat16 [8, 16, 2, 24, 128, 128], P('row', 'col', 'layer'), may hold values from -1.1953125 to 1.1953125
- a_pos: int32 [8, 16, 2, 24], P('row', 'col', 'layer'), may hold values from 0 to 31, as said below
- a_count: int32 [8, 16, 2], P('row', 'col', 'layer'), may hold values from 6 to 24
- b_vals: bfloat16 [8, 16, 2, 2, 6, 128, 128], P('row', 'col', 'layer'), may hold values from -1.1953125 to 1.1953125
- b_pos: int32 [8, 16, 2, 2, 6], P('row', 'col', 'layer'), may hold values from 0 to 31, as said below
- b_count: int32 [8, 16, 2, 2], P('row', 'col', 'layer'), may hold values from 1 to 6
Outputs:
- product: float32 [8192, 16384], P('row', ('col', 'layer'))
The draws below stay inside these ranges and needn't reach their ends.
Inputs may be any that keep to these rules, and one draw needn't show every extreme that they name: `a_pos`: within one panel (fixed first three indices) the 24 entries are distinct. `b_pos`: within one panel (fixed first four indices) the 6 entries are distinct.
All inputs are finite; a program needn't handle non-finite values.
Results may differ from the reference program's by a relative error of at most 0.0003.
Values may be sent and summed in bfloat16 or wider, within the bound.
No kernel may reach another device: no remote copies, remote signals or barrier semaphores. Data moves between devices by JAX's collectives and lax.ppermute only.
A program may use at most 64 MiB of HBM per device.

```python
import jax
import jax.numpy as jnp
from jax import lax

BLOCK = 128
KB = 4
CB = 8
RB = 8
SB = 6
SA = 24
PR = 8
PC = 16
PL = 2
HB = 2
NR = 64
NC = 128


def first_slots(key, panels, span, keep):
    keys = jax.random.split(key, panels)
    orders = jax.vmap(lambda one: jax.random.permutation(one, span))(keys)
    return orders[:, :keep].astype(jnp.int32)


def filled_counts(key, panels, lowest, most):
    first, second = jax.random.split(key)
    counts = jax.random.randint(first, (panels,), lowest, most + 1, dtype=jnp.int32)
    where = jax.random.randint(second, (), 0, panels, dtype=jnp.int32)
    return counts.at[where].set(most)


def draw_a_pos(key, part):
    key = jax.random.fold_in(key, 11)
    slots = first_slots(key, PR * PC * PL, RB * KB, SA)
    return slots.reshape(PR, PC, PL, SA)


def draw_a_count(key, part):
    key = jax.random.fold_in(key, 12)
    counts = filled_counts(key, PR * PC * PL, max(SA // 4, 1), SA)
    return counts.reshape(PR, PC, PL)


def draw_b_pos(key, part):
    key = jax.random.fold_in(key, 13)
    slots = first_slots(key, PR * PC * PL * HB, KB * CB, SB)
    return slots.reshape(PR, PC, PL, HB, SB)


def draw_b_count(key, part):
    key = jax.random.fold_in(key, 14)
    counts = filled_counts(key, PR * PC * PL * HB, 1, SB)
    return counts.reshape(PR, PC, PL, HB)


def level_of(rng, dims, pieces, least, top_value):
    def one(dim, shards_of):
        steps = jax.random.uniform(jax.random.fold_in(jax.random.fold_in(rng, 6), dim), (shards_of,), jnp.float32, least / len(pieces), top_value / len(pieces))
        return jnp.repeat(jnp.exp(steps), dims[dim] // shards_of).reshape((-1,) + (1,) * (len(dims) - dim - 1))

    gain = one(*pieces[0])
    for cut in pieces[1:]:
        gain = gain * one(*cut)
    return gain


def gaussian(rng, extent, scale, limit, cuts=(), held_as=jnp.bfloat16):
    level = level_of(rng, extent, cuts, -0.22, 0.18) if cuts else 1.0
    entries = jax.random.normal(rng, extent, jnp.float32) * scale * level
    return jnp.minimum(jnp.maximum(entries, -limit), limit).astype(held_as)


def setup_inputs(seed: int = 0) -> dict:
    key_list = jax.random.split(jax.random.key(seed), 7)
    a_vals = gaussian(key_list[0], (PR, PC, PL, SA, BLOCK, BLOCK), 0.2, 1.1953125, ((0, 8), (1, 16), (2, 2)))
    a_pos = draw_a_pos(jax.random.fold_in(key_list[6], 71), 0)
    a_count = draw_a_count(jax.random.fold_in(key_list[6], 71), 0)
    b_vals = gaussian(key_list[3], (PR, PC, PL, HB, SB, BLOCK, BLOCK), 0.2, 1.1953125, ((0, 8), (1, 16), (2, 2)))
    b_pos = draw_b_pos(jax.random.fold_in(key_list[6], 71), 0)
    b_count = draw_b_count(jax.random.fold_in(key_list[6], 71), 0)
    return {"a_vals": a_vals, "a_pos": a_pos, "a_count": a_count, "b_vals": b_vals, "b_pos": b_pos, "b_count": b_count}


def contribute(total, a_vals, a_pos, a_count, b_vals, b_pos, b_count):
    block = a_vals.shape[-1]
    slots_a = a_vals.shape[0]
    target = (a_pos % KB) * RB + a_pos // KB
    live_a = jnp.arange(slots_a, dtype=jnp.int32) < a_count
    places = jnp.arange(KB * RB, dtype=jnp.int32)
    select = ((target[:, None] == places[None, :]) & live_a[:, None]).astype(jnp.float32)
    placed = jnp.einsum("sp,sab->pab", select, a_vals.astype(jnp.float32)).astype(jnp.bfloat16)
    columns = placed.reshape(KB, RB * block, block)
    for slot in range(b_vals.shape[0]):
        entry = b_pos[slot]
        left = lax.dynamic_index_in_dim(columns, entry // CB, 0, keepdims=False)
        term = jnp.dot(left, b_vals[slot], preferred_element_type=jnp.float32)
        live = (slot < b_count).astype(jnp.float32)
        start = (entry % CB) * block
        old = lax.dynamic_slice_in_dim(total, start, block, 1)
        total = lax.dynamic_update_slice_in_dim(total, old + live * term, start, 1)
    return total


def reference(a_vals, a_pos, a_count, b_vals, b_pos, b_count):
    height = RB * BLOCK
    breadth = CB * BLOCK

    def one_panel(index):
        row_i = index // PC
        col_j = index % PC

        def one_turn(total, turn):
            group = turn // PC
            local = turn % PC
            a_col = (local - row_i) % PC
            b_row = (local - col_j) % PR
            stack = local // PR
            total = contribute(total, a_vals[row_i, a_col, group], a_pos[row_i, a_col, group],
                               a_count[row_i, a_col, group], b_vals[b_row, col_j, group, stack],
                               b_pos[b_row, col_j, group, stack], b_count[b_row, col_j, group, stack])
            return total, None

        start = jnp.zeros((height, breadth), jnp.float32)
        total, _ = lax.scan(one_turn, start, jnp.arange(PL * PC, dtype=jnp.int32))
        return total

    panels = lax.map(one_panel, jnp.arange(PR * PC, dtype=jnp.int32))
    panels = panels.reshape(PR, PC, height, breadth).transpose(0, 2, 1, 3)
    return panels.reshape(NR * BLOCK, NC * BLOCK)
```

```python
import functools

import jax
import jax.numpy as jnp
from jax import lax
from jax.experimental import pallas as pl
from jax.experimental.pallas import tpu as pltpu
from jax.sharding import Mesh
from jax.sharding import PartitionSpec as P

BLOCK = 128
KB = 4
CB = 8
RB = 8
SA = 24
SB = 6
FIRST = 16
LATER = SA - FIRST
HALF = RB // 2
META = 16
ROWS_1 = FIRST * BLOCK + META
ROWS_2 = LATER * BLOCK
ROWS_B = 2 * SB * BLOCK + META
OFFSETS = (0, -1, 1, -2, 2, -3, 3, 4)
HEIGHT = HALF * BLOCK
NEAR = (0, 1, 2, 3, 4)
FAR = (5, 6, 7)
STEPS = 64.0
TOP = 32760.0
LOWEST = -120.0
GRANT = 56 * 1024 * 1024

ANY = pl.BlockSpec(memory_space=pl.ANY)
SMEM = pl.BlockSpec(memory_space=pltpu.SMEM)
VMEM = pl.BlockSpec(memory_space=pltpu.VMEM)


def pack_kernel(a_pos, a_count, b_pos, b_count, a_vals, b_vals, p1, p2, pb, place):
    pb[: 2 * SB * BLOCK, :] = b_vals[...]
    p1[...] = jnp.zeros_like(p1)
    p2[...] = jnp.zeros_like(p2)
    for p in range(KB * RB):
        place[p] = -1
    for s in range(SA):
        place[a_pos[s]] = jnp.where(s < a_count[0], s, -1)
    lane = lax.broadcasted_iota(jnp.int32, (META, BLOCK), 1)

    def send(p, carry):
        rank, low, words = carry
        slot = place[p]
        live = slot >= 0
        start = pl.ds(pl.multiple_of(jnp.maximum(slot, 0) * BLOCK, BLOCK), BLOCK)

        @pl.when(live & (rank < FIRST))
        def _():
            p1[pl.ds(pl.multiple_of(rank * BLOCK, BLOCK), BLOCK), :] = a_vals[start, :]

        @pl.when(live & (rank >= FIRST))
        def _():
            p2[pl.ds(pl.multiple_of((rank - FIRST) * BLOCK, BLOCK), BLOCK), :] = a_vals[start, :]

        one = live.astype(jnp.int32)
        words = jnp.where((lane == rank) & live, p, words)
        return rank + one, low + jnp.where(p < HALF * KB, one, 0), words

    words = jnp.zeros((META, BLOCK), jnp.int32)
    total, low, words = lax.fori_loop(0, KB * RB, send, (jnp.int32(0), jnp.int32(0), words))
    words = jnp.where(lane == SA, low, words)
    words = jnp.where(lane == SA + 1, total, words)
    p1[FIRST * BLOCK :, :] = words.astype(jnp.float32).astype(jnp.bfloat16)
    words = jnp.zeros((META, BLOCK), jnp.int32)
    for h in range(2):
        for s in range(SB):
            words = jnp.where(lane == h * SB + s, b_pos[h, s], words)
        words = jnp.where(lane == 2 * SB + h, b_count[h], words)
    pb[2 * SB * BLOCK :, :] = words.astype(jnp.float32).astype(jnp.bfloat16)


def pack(a_pos, a_count, b_pos, b_count, a_vals, b_vals):
    return pl.pallas_call(
        pack_kernel,
        out_shape=[
            jax.ShapeDtypeStruct((ROWS_1, BLOCK), jnp.bfloat16),
            jax.ShapeDtypeStruct((ROWS_2, BLOCK), jnp.bfloat16),
            jax.ShapeDtypeStruct((ROWS_B, BLOCK), jnp.bfloat16),
        ],
        in_specs=[SMEM, SMEM, SMEM, SMEM, VMEM, VMEM],
        out_specs=[VMEM, VMEM, VMEM],
        scratch_shapes=[pltpu.SMEM((KB * RB,), jnp.int32)],
        name="pack",
    )(a_pos, a_count, b_pos, b_count, a_vals, b_vals)


def x_distances(p):
    offset = OFFSETS[p]
    if offset % 2 == 0:
        return (offset // 2 % 4,)
    return ((offset - 1) // 2 % 4, (offset + 1) // 2 % 4)


def wanted(panels):
    lists = [x_distances(p) for p in panels]
    same = sorted({d for one in lists if len(one) == 1 for d in one})
    other = sorted({d for one in lists if len(one) == 2 for d in one})
    return same, other


def product_kernel(upper, panels, first, last, place, *refs):
    count = len(panels)
    refs = list(refs)
    ones = {p: [refs.pop(0) for _ in range(1 if p < 7 else 2)] for p in panels}
    twos = {p: [refs.pop(0) for _ in range(1 if p < 7 else 2)] for p in panels} if upper else {}
    same_wanted, other_wanted = wanted(panels)
    same = {d: refs.pop(0) for d in same_wanted}
    other = {d: refs.pop(0) for d in other_wanted}
    acc_in = None if first else refs.pop(0)
    outs = [refs.pop(0) for _ in range(4 if last else 1)]
    a_buf, a_buf2, b_buf, dense, acc, meta, words, said = refs[:8]
    sem_a, sem_a2, sem_b, sem_am, sem_bm, sem_w = refs[8:]
    i, core, yl, z, yh = (place[k] for k in range(5))

    def whole(of, buf, sem, n, split):
        if len(of) == 1:
            return [pltpu.make_async_copy(of[0], buf.at[n], sem.at[n])]
        rest = buf.shape[1] - split
        return [
            pltpu.make_async_copy(of[0], buf.at[n, pl.ds(0, split)], sem.at[n]),
            pltpu.make_async_copy(of[1], buf.at[n, pl.ds(split, rest)], sem.at[count]),
        ]

    def a_copies(n, p):
        copies = whole(ones[p], a_buf, sem_a, n, FIRST // 2 * BLOCK)
        if upper:
            copies += whole(twos[p], a_buf2, sem_a2, n, LATER // 2 * BLOCK)
        return copies

    def a_meta(n, p):
        of = ones[p][-1]
        return pltpu.make_async_copy(of.at[pl.ds(of.shape[0] - META, META)], meta.at[n], sem_am.at[n])

    def b_source(p):
        distances = x_distances(p)
        if len(distances) == 1:
            return [(None, same[distances[0]])]
        return [(c, other[d]) for c, d in enumerate(distances)]

    def b_meta(n, p, group, of):
        k = n * 2 + group
        start = group * ROWS_B + 2 * SB * BLOCK
        return pltpu.make_async_copy(of.at[pl.ds(start, META)], meta.at[count + k], sem_bm.at[k])

    def stack(p):
        residue = lax.rem(i + z + OFFSETS[p] + 8, 8)
        return jnp.where(residue < i, 1 - yl, yl)

    def b_copy(n, p, group, of):
        start = pl.multiple_of(group * ROWS_B + stack(p) * (SB * BLOCK), META)
        return pltpu.make_async_copy(of.at[pl.ds(start, SB * BLOCK)], b_buf.at[n, group], sem_b.at[n * 2 + group])

    def each_b(make):
        for n, p in enumerate(panels):
            for group in range(2):
                for when, of in b_source(p):
                    if when is None:
                        make(n, p, group, of).start()
                    else:

                        @pl.when(core == when)
                        def _(n=n, p=p, group=group, of=of):
                            make(n, p, group, of).start()

    for n, p in enumerate(panels):
        a_meta(n, p).start()
    each_b(b_meta)
    if not first:
        acc_copy = pltpu.make_async_copy(acc_in, acc, sem_w.at[1])
        acc_copy.start()
    for n, p in enumerate(panels):
        for copy in a_copies(n, p):
            copy.start()
    each_b(b_copy)

    for n, p in enumerate(panels):
        a_meta(n, p).wait()
        for group in range(2):
            b_meta(n, p, group, b_source(p)[0][1]).wait()
    for k in range(3 * count):
        words[pl.ds(k, 1), :] = meta[k].astype(jnp.float32)[:1].astype(jnp.int32)
    to_scalars = pltpu.make_async_copy(words, said, sem_w.at[0])
    to_scalars.start()
    dense[...] = jnp.zeros_like(dense)
    if first:
        acc[...] = jnp.zeros_like(acc)
    to_scalars.wait()
    if not first:
        acc_copy.wait()

    blank = jnp.zeros((BLOCK, BLOCK), jnp.bfloat16)
    for n, p in enumerate(panels):
        for copy in a_copies(n, p):
            copy.wait()
        for group in range(2):
            b_copy(n, p, group, b_source(p)[0][1]).wait()

        def put(s, carry, source, skip, n=n):
            at = said[n, s]
            row = lax.shift_right_logical(at, 2) - (HALF if upper else 0)
            to = pl.multiple_of(row * BLOCK, BLOCK)
            start = pl.multiple_of((s - skip) * BLOCK, BLOCK)
            dense[n, lax.rem(at, KB), pl.ds(to, BLOCK), :] = source[n, pl.ds(start, BLOCK), :]
            return carry

        low, total = said[n, SA], said[n, SA + 1]
        if upper:
            lax.fori_loop(low, jnp.minimum(total, FIRST), functools.partial(put, source=a_buf, skip=0), 0)
            lax.fori_loop(FIRST, total, functools.partial(put, source=a_buf2, skip=FIRST), 0)
        else:
            lax.fori_loop(0, low, functools.partial(put, source=a_buf, skip=0), 0)

        h = stack(p)
        for s in range(SB):
            for group in range(2):
                k = count + 2 * n + group
                at = said[k, h * SB + s]
                live = s < said[k, 2 * SB + h]
                right = jnp.where(live, b_buf[n, group, s * BLOCK : (s + 1) * BLOCK, :], blank)
                left = dense[n, lax.shift_right_logical(at, 3)]
                acc[group * CB + lax.rem(at, CB)] += jnp.dot(left, right, preferred_element_type=jnp.float32)

    if not last:
        out_copy = pltpu.make_async_copy(acc, outs[0], sem_w.at[2])
        out_copy.start()
        out_copy.wait()
        return
    own_out, q2_out, qp_out, qm_out = outs
    for c in range(CB // 2):
        own_out[:, c * BLOCK : (c + 1) * BLOCK] = acc[yh * (CB // 2) + c]
    row = lax.broadcasted_iota(jnp.int32, (META, BLOCK), 0)
    for q_out, group, side in (
        (q2_out, 0, 1 - yh),
        (qp_out, 1, jnp.where(yl == 1, 1 - yh, yh)),
        (qm_out, 1, jnp.where(yl == 1, yh, 1 - yh)),
    ):
        for c in range(CB // 2):
            columns = slice(c * BLOCK, (c + 1) * BLOCK)
            codes = jnp.zeros((META, BLOCK), jnp.float32)
            for r in range(HALF):
                rows = slice(r * BLOCK, (r + 1) * BLOCK)
                value = acc[group * CB + side * (CB // 2) + c, rows, :]
                peak = jnp.max(jnp.max(jnp.abs(value), axis=0, keepdims=True), axis=1, keepdims=True)
                code = jnp.ceil(jnp.maximum(jnp.log2(peak), LOWEST) * STEPS)
                scaled = value * (TOP * jnp.exp2(code * (-1.0 / STEPS)))
                q_out[rows, columns] = jnp.round(scaled).astype(jnp.int32).astype(jnp.int16)
                codes = jnp.where(row == r, code, codes)
            q_out[HEIGHT:, columns] = codes.astype(jnp.int32).astype(jnp.int16)


def product(upper, panels, place, ones, twos, same, other, so_far, last):
    sent = jax.ShapeDtypeStruct((HEIGHT + META, CB // 2 * BLOCK), jnp.int16)
    count = len(panels)

    def picked(of):
        return [one for p in panels for one in (of[p : p + 1] if p < 7 else of[7:9])]

    arrays = picked(ones) + (picked(twos) if upper else [])
    same_wanted, other_wanted = wanted(panels)
    arrays += [same[d] for d in same_wanted] + [other[d] for d in other_wanted]
    first = so_far is None
    if not first:
        arrays.append(so_far)
    if last:
        outs = [jax.ShapeDtypeStruct((HEIGHT, CB // 2 * BLOCK), jnp.float32), sent, sent, sent]
    else:
        outs = jax.ShapeDtypeStruct((2 * CB, HEIGHT, BLOCK), jnp.float32)
    return pl.pallas_call(
        functools.partial(product_kernel, upper, panels, first, last),
        out_shape=outs,
        in_specs=[SMEM] + [ANY] * len(arrays),
        out_specs=[VMEM] * 4 if last else ANY,
        scratch_shapes=[
            pltpu.VMEM((count, ROWS_1, BLOCK), jnp.bfloat16),
            pltpu.VMEM((count, ROWS_2, BLOCK) if upper else (1, META, BLOCK), jnp.bfloat16),
            pltpu.VMEM((count, 2, SB * BLOCK, BLOCK), jnp.bfloat16),
            pltpu.VMEM((count, KB, HEIGHT, BLOCK), jnp.bfloat16),
            pltpu.VMEM((2 * CB, HEIGHT, BLOCK), jnp.float32),
            pltpu.VMEM((3 * count, META, BLOCK), jnp.bfloat16),
            pltpu.VMEM((24, BLOCK), jnp.int32),
            pltpu.SMEM((24, BLOCK), jnp.int32),
            pltpu.SemaphoreType.DMA((count + 1,)),
            pltpu.SemaphoreType.DMA((count + 1,)),
            pltpu.SemaphoreType.DMA((2 * count,)),
            pltpu.SemaphoreType.DMA((count,)),
            pltpu.SemaphoreType.DMA((2 * count,)),
            pltpu.SemaphoreType.DMA((3,)),
        ],
        compiler_params=pltpu.CompilerParams(vmem_limit_bytes=GRANT),
        cost_estimate=pl.CostEstimate(flops=1_000_000_000 * count, bytes_accessed=2_000_000 * count, transcendentals=0),
        name=("upper" if upper else "lower") + ("_last" if last else "_first"),
    )(place, *arrays)


def sum_kernel(*refs):
    own, parts, out = refs[0], refs[1:7], refs[-1]
    r = pl.program_id(0)
    row = lax.broadcasted_iota(jnp.int32, (META, CB // 2 * BLOCK), 0)
    total = own[...]
    for value, codes in zip(parts[:3], parts[3:]):
        code = jnp.where(row == r, codes[...].astype(jnp.int32).astype(jnp.float32), 0.0)
        scale = jnp.exp2(jnp.sum(code, axis=0, keepdims=True) * (1.0 / STEPS)) * (1.0 / TOP)
        total = total + value[...].astype(jnp.int32).astype(jnp.float32) * scale
    out[...] = total


def add_up(own, parts, so_far):
    width = CB // 2 * BLOCK
    skip = 0 if so_far is None else HALF
    values = pl.BlockSpec((BLOCK, width), lambda r: (r, 0))
    codes = pl.BlockSpec((META, width), lambda r: (HEIGHT // META, 0))
    extra = () if so_far is None else (so_far,)
    return pl.pallas_call(
        sum_kernel,
        grid=(HALF,),
        out_shape=jax.ShapeDtypeStruct((RB * BLOCK, width), jnp.float32),
        in_specs=[values] + [values] * 3 + [codes] * 3 + [ANY] * len(extra),
        out_specs=pl.BlockSpec((BLOCK, width), lambda r: (r + skip, 0)),
        input_output_aliases={7: 0} if extra else {},
        name="add_up",
    )(own, *parts, *parts, *extra)


def shift(value, axis, distance):
    size = lax.axis_size(axis)
    return lax.ppermute(value, axis, [(k, (k + distance) % size) for k in range(size)])


def shift_y(value, distance):
    pairs = []
    for y in range(4):
        to = (y + distance) % 4
        pairs.append((y % 2 * 2 + y // 2, to % 2 * 2 + to // 2))
    return lax.ppermute(value, ("yl", "yh"), pairs)


def round_z(own, split, after=None):
    up, down, ups, downs = own, own, [], []
    for step in range(3):
        if step == 1 and after is not None:
            up, down, _ = lax.optimization_barrier((up, down, after))
        up, down = shift(up, "z", 1), shift(down, "z", -1)
        ups.append(up)
        downs.append(down)
    opposite = [shift(up[:split], "z", 1), shift(down[split:], "z", -1)]
    return [own, ups[0], downs[0], ups[1], downs[1], ups[2], downs[2], *opposite]


def per_device(a_vals, a_pos, a_count, b_vals, b_pos, b_count):
    place = jnp.stack(
        [
            lax.axis_index("x") * 2 + lax.axis_index("core"),
            lax.axis_index("core"),
            lax.axis_index("yl"),
            lax.axis_index("z"),
            lax.axis_index("yh"),
        ]
    ).astype(jnp.int32)
    p1, p2, pb = pack(
        a_pos.reshape(SA),
        a_count.reshape(1),
        b_pos.reshape(2, SB),
        b_count.reshape(2),
        a_vals.reshape(SA * BLOCK, BLOCK),
        b_vals.reshape(2 * SB * BLOCK, BLOCK),
    )
    both = jnp.concatenate([pb, shift(pb, "yl", 1)], axis=0)
    after, before = shift(both, "x", -1), shift(both, "x", 1)
    late, _, _ = lax.optimization_barrier((both, after, before))
    same = [both, after, shift(late, "x", 2), before]
    other = [shift(one, "core", 1) for one in same]
    ones = round_z(p1, FIRST // 2 * BLOCK)
    p2, _ = lax.optimization_barrier((p2, ones[6]))

    def half(upper, twos):
        so_far = product(upper, NEAR, place, ones, twos, same, other, None, False)
        own, q2, qp, qm = product(upper, FAR, place, ones, twos, same, other, so_far, True)
        return own, (shift_y(q2, 2), shift_y(qp, 1), shift_y(qm, -1)), q2

    own1, parts1, done = half(False, None)
    twos = round_z(p2, LATER // 2 * BLOCK, done)
    own2, parts2, _ = half(True, twos)
    return add_up(own2, parts2, add_up(own1, parts1, None))


def solution(mesh):
    cores = 2
    x = mesh.shape["row"] // cores
    z = mesh.shape["col"] // 2
    split = Mesh(mesh.devices.reshape(x, cores, 2, z, mesh.shape["layer"]), ("x", "core", "yl", "z", "yh"))
    lead = (("x", "core"), ("yl", "z"), "yh")
    return jax.shard_map(
        per_device,
        mesh=split,
        in_specs=(P(*lead), P(*lead), P(*lead), P(*lead), P(*lead), P(*lead)),
        out_specs=P(("x", "core"), ("yl", "z", "yh")),
        check_vma=False,
    )
```

```python
import functools
import math

import jax
import jax.numpy as jnp
from jax import lax
from jax.experimental import pallas as pl
from jax.experimental.pallas import tpu as pltpu
from jax.sharding import Mesh
from jax.sharding import PartitionSpec as P

BLOCK = 128
KB = 4
CB = 8
RB = 8
SA = 24
SB = 6
HALF = RB // 2
META = 16
SPARE = 64
ROWS_A = SA * BLOCK + SPARE + META
ROWS_B = SB * BLOCK + META
OFFSETS = (0, -1, 1, -2, 2, -3, 3, 4)
HEIGHT = HALF * BLOCK
ROW = ("x", "core")
NEAR = (0, 1, 2)
NEXT = (3, 4)
FAR = (5, 6, 7)
STEPS = 64.0
TOP = 32760.0
LOWEST = -120.0
MIB = 1024 * 1024

HBM = pl.BlockSpec(memory_space=pltpu.HBM)
ANY = pl.BlockSpec(memory_space=pl.ANY)
SMEM = pl.BlockSpec(memory_space=pltpu.SMEM)
VMEM = pl.BlockSpec(memory_space=pltpu.VMEM)


def pack_kernel(a_pos, a_count, b_pos, b_count, a_vals, b_vals, pa, pb, place):
    lane = lax.broadcasted_iota(jnp.int32, (META, BLOCK), 1)
    for h in range(2):
        start = h * ROWS_B
        pb[start : start + SB * BLOCK, :] = b_vals[h * SB * BLOCK : (h + 1) * SB * BLOCK, :]
        words = jnp.zeros((META, BLOCK), jnp.int32)
        for s in range(SB):
            words = jnp.where(lane == s, b_pos[h, s], words)
        words = jnp.where(lane == SB, b_count[h], words)
        pb[start + SB * BLOCK : start + ROWS_B, :] = words.astype(jnp.float32).astype(jnp.bfloat16)
    pa[...] = jnp.zeros_like(pa)
    for p in range(KB * RB):
        place[p] = -1
    for s in range(SA):
        place[a_pos[s]] = jnp.where(s < a_count[0], s, -1)

    def send(p, carry):
        rank, low, words = carry
        slot = place[p]
        live = slot >= 0
        start = pl.ds(pl.multiple_of(jnp.maximum(slot, 0) * BLOCK, BLOCK), BLOCK)

        @pl.when(live)
        def _():
            pa[pl.ds(pl.multiple_of(rank * BLOCK, BLOCK), BLOCK), :] = a_vals[start, :]

        one = live.astype(jnp.int32)
        words = jnp.where((lane == rank) & live, p, words)
        return rank + one, low + jnp.where(p < HALF * KB, one, 0), words

    words = jnp.zeros((META, BLOCK), jnp.int32)
    total, low, words = lax.fori_loop(0, KB * RB, send, (jnp.int32(0), jnp.int32(0), words))
    words = jnp.where(lane == SA, low, words)
    words = jnp.where(lane == SA + 1, total, words)
    pa[ROWS_A - META :, :] = words.astype(jnp.float32).astype(jnp.bfloat16)


def pack(a_pos, a_count, b_pos, b_count, a_vals, b_vals):
    return pl.pallas_call(
        pack_kernel,
        out_shape=[
            jax.ShapeDtypeStruct((ROWS_A, BLOCK), jnp.bfloat16),
            jax.ShapeDtypeStruct((2 * ROWS_B, BLOCK), jnp.bfloat16),
        ],
        in_specs=[SMEM, SMEM, SMEM, SMEM, VMEM, VMEM],
        out_specs=[VMEM] * 2,
        scratch_shapes=[pltpu.SMEM((KB * RB,), jnp.int32)],
        name="pack",
    )(a_pos, a_count, b_pos, b_count, a_vals, b_vals)


def product_kernel(upper, panels, first, last, place, *refs):
    count = len(panels)
    refs = list(refs)
    density = {p: refs.pop(0) for p in panels}
    gram = {p: [refs.pop(0) for _ in range(1 if p < 7 else 2)] for p in panels}
    so_far = refs.pop(0) if upper else None
    acc_in = None if first else refs.pop(0)
    outs = [refs.pop(0) for _ in range(4 if last else 1)]
    a_buf, b_buf, dense, acc, meta, words, said = refs[:7]
    sem_a, sem_b, sem_am, sem_bm, sem_w = refs[7:]
    yl, yh, i, z = (place[k] for k in range(4))

    def a_copy(n, p):
        return pltpu.make_async_copy(density[p], a_buf.at[n], sem_a.at[n])

    def a_meta(n, p):
        return pltpu.make_async_copy(density[p].at[pl.ds(ROWS_A - META, META)], meta.at[n], sem_am.at[n])

    def gram_rows(p, group, start, rows):
        residue = lax.rem(i + z + OFFSETS[p] + 8, 8)
        stack = jnp.where(residue < i, 1 - yl, yl)
        start = (group * 2 * (2 - len(gram[p])) + stack) * ROWS_B + start
        return gram[p][group % len(gram[p])].at[pl.ds(pl.multiple_of(start, META), rows)]

    def b_meta(n, p, group):
        k = n * 2 + group
        return pltpu.make_async_copy(gram_rows(p, group, SB * BLOCK, META), meta.at[count + k], sem_bm.at[k])

    def b_copy(n, p, group):
        source = gram_rows(p, group, 0, SB * BLOCK)
        return pltpu.make_async_copy(source, b_buf.at[n, group], sem_b.at[n * 2 + group])

    for n, p in enumerate(panels):
        a_meta(n, p).start()
        for group in range(2):
            b_meta(n, p, group).start()
    if not first:
        acc_copy = pltpu.make_async_copy(acc_in, acc, sem_w.at[1])
        acc_copy.start()
    for n, p in enumerate(panels):
        a_copy(n, p).start()
        for group in range(2):
            b_copy(n, p, group).start()

    for n, p in enumerate(panels):
        a_meta(n, p).wait()
        for group in range(2):
            b_meta(n, p, group).wait()
    for k in range(3 * count):
        words[pl.ds(k, 1), :] = meta[k].astype(jnp.float32)[:1].astype(jnp.int32)
    to_scalars = pltpu.make_async_copy(words, said, sem_w.at[0])
    to_scalars.start()
    dense[...] = jnp.zeros_like(dense)
    if first:
        acc[...] = jnp.zeros_like(acc)
    to_scalars.wait()
    if not first:
        acc_copy.wait()

    blank = jnp.zeros((BLOCK, BLOCK), jnp.bfloat16)
    for n, p in enumerate(panels):
        a_copy(n, p).wait()
        for group in range(2):
            b_copy(n, p, group).wait()

        def put(s, carry, n=n):
            at = said[n, s]
            row = lax.shift_right_logical(at, 2) - (HALF if upper else 0)
            to = pl.multiple_of(row * BLOCK, BLOCK)
            start = pl.multiple_of(s * BLOCK, BLOCK)
            dense[n, lax.rem(at, KB), pl.ds(to, BLOCK), :] = a_buf[n, pl.ds(start, BLOCK), :]
            return carry

        low, total = said[n, SA], said[n, SA + 1]
        lax.fori_loop(*((low, total) if upper else (0, low)), put, 0)

        for s in range(SB):
            for group in range(2):
                k = count + 2 * n + group
                at = said[k, s]
                live = s < said[k, SB]
                right = jnp.where(live, b_buf[n, group, s * BLOCK : (s + 1) * BLOCK, :], blank)
                left = dense[n, lax.shift_right_logical(at, 3)]
                acc[group * CB + lax.rem(at, CB)] += jnp.dot(left, right, preferred_element_type=jnp.float32)

    if not last:
        out_copy = pltpu.make_async_copy(acc, outs[0], sem_w.at[2])
        out_copy.start()
        out_copy.wait()
        return
    own_out, q2_out, qp_out, qm_out = outs
    rows = pl.ds(HEIGHT if upper else 0, HEIGHT)
    own_copies = [
        pltpu.make_async_copy(acc.at[yh * (CB // 2) + c], own_out.at[rows, pl.ds(c * BLOCK, BLOCK)], sem_w.at[3 + c])
        for c in range(CB // 2)
    ]
    for copy in own_copies:
        copy.start()
    row = lax.broadcasted_iota(jnp.int32, (META, BLOCK), 0)
    for q_out, group, side in (
        (q2_out, 0, 1 - yh),
        (qp_out, 1, jnp.where(yl == 1, 1 - yh, yh)),
        (qm_out, 1, jnp.where(yl == 1, yh, 1 - yh)),
    ):
        for c in range(CB // 2):
            columns = slice(c * BLOCK, (c + 1) * BLOCK)
            codes = jnp.zeros((META, BLOCK), jnp.float32)
            for r in range(HALF):
                rows = slice(r * BLOCK, (r + 1) * BLOCK)
                value = acc[group * CB + side * (CB // 2) + c, rows, :]
                peak = jnp.max(jnp.max(jnp.abs(value), axis=0, keepdims=True), axis=1, keepdims=True)
                code = jnp.ceil(jnp.maximum(jnp.log2(peak), LOWEST) * STEPS)
                scaled = value * (TOP * jnp.exp2(code * (-1.0 / STEPS)))
                q_out[rows, columns] = jnp.round(scaled).astype(jnp.int32).astype(jnp.int16)
                codes = jnp.where(row == r, code, codes)
            q_out[HEIGHT:, columns] = codes.astype(jnp.int32).astype(jnp.int16)
    for copy in own_copies:
        copy.wait()


def product(upper, panels, place, density, gram, so_far, last, out=None):
    sent = jax.ShapeDtypeStruct((HEIGHT + META, CB // 2 * BLOCK), jnp.int16)
    count = len(panels)
    arrays = [density[p] for p in panels] + [one for p in panels for one in (gram[p : p + 1] if p < 7 else gram[7:9])]
    if upper:
        arrays.append(out)
    first = so_far is None
    if not first:
        arrays.append(so_far)
    if last:
        outs = [jax.ShapeDtypeStruct((RB * BLOCK, CB // 2 * BLOCK), jnp.float32), sent, sent, sent]
    else:
        outs = jax.ShapeDtypeStruct((2 * CB, HEIGHT, BLOCK), jnp.float32)
    return pl.pallas_call(
        functools.partial(product_kernel, upper, panels, first, last),
        out_shape=outs,
        in_specs=[SMEM] + [HBM] * (len(arrays) - (not first)) + [ANY] * (not first),
        out_specs=[HBM, VMEM, VMEM, VMEM] if last else ANY,
        input_output_aliases={len(arrays): 0} if upper else {},
        scratch_shapes=[
            pltpu.VMEM((count, ROWS_A, BLOCK), jnp.bfloat16),
            pltpu.VMEM((count, 2, SB * BLOCK, BLOCK), jnp.bfloat16),
            pltpu.VMEM((count, KB, HEIGHT, BLOCK), jnp.bfloat16),
            pltpu.VMEM((2 * CB, HEIGHT, BLOCK), jnp.float32),
            pltpu.VMEM((3 * count, META, BLOCK), jnp.bfloat16),
            pltpu.VMEM((24, BLOCK), jnp.int32),
            pltpu.SMEM((24, BLOCK), jnp.int32),
            pltpu.SemaphoreType.DMA((count,)),
            pltpu.SemaphoreType.DMA((2 * count,)),
            pltpu.SemaphoreType.DMA((count,)),
            pltpu.SemaphoreType.DMA((2 * count,)),
            pltpu.SemaphoreType.DMA((3 + CB // 2,)),
        ],
        compiler_params=pltpu.CompilerParams(vmem_limit_bytes=(8 + 2 * count) * MIB),
        cost_estimate=pl.CostEstimate(flops=1_000_000_000 * count, bytes_accessed=2_000_000 * count, transcendentals=0),
        name=("upper" if upper else "lower") + str(count) + ("_last" if last else ""),
    )(place, *arrays)


def sum_kernel(skip, *refs):
    parts, so_far, out, own, got, sem_part, sem_in, sem_out = refs[:3], *refs[3:]

    def part(k, r):
        rows = pl.ds(r * BLOCK, BLOCK if r < HALF else META)
        return pltpu.make_async_copy(parts[k].at[rows], got.at[k, rows], sem_part.at[k, r])

    def read(r):
        rows = pl.ds(r * BLOCK, BLOCK)
        return pltpu.make_async_copy(so_far.at[pl.ds((skip + r) * BLOCK, BLOCK)], own.at[rows], sem_in.at[r])

    def write(r):
        rows = pl.ds(r * BLOCK, BLOCK)
        return pltpu.make_async_copy(own.at[rows], out.at[pl.ds((skip + r) * BLOCK, BLOCK)], sem_out.at[r])

    for r in (HALF, *range(HALF)):
        for k in range(3):
            part(k, r).start()
        if r < HALF:
            read(r).start()
    scales = []
    for k in range(3):
        part(k, HALF).wait()
        codes = got[k, HEIGHT:, :].astype(jnp.int32).astype(jnp.float32)
        scales.append(jnp.exp2(codes * (1.0 / STEPS)) * (1.0 / TOP))
    for r in range(HALF):
        rows = pl.ds(r * BLOCK, BLOCK)
        read(r).wait()
        value = own[rows, :]
        for k in range(3):
            part(k, r).wait()
            value = value + got[k, rows, :].astype(jnp.int32).astype(jnp.float32) * scales[k][r : r + 1]
        own[rows, :] = value
        write(r).start()
    for r in range(HALF):
        write(r).wait()


def add_up(upper, parts, so_far):
    width = CB // 2 * BLOCK
    return pl.pallas_call(
        functools.partial(sum_kernel, HALF if upper else 0),
        out_shape=jax.ShapeDtypeStruct((RB * BLOCK, width), jnp.float32),
        in_specs=[ANY] * 3 + [HBM],
        out_specs=HBM,
        input_output_aliases={3: 0},
        scratch_shapes=[
            pltpu.VMEM((HEIGHT, width), jnp.float32),
            pltpu.VMEM((3, HEIGHT + META, width), jnp.int16),
            pltpu.SemaphoreType.DMA((3, HALF + 1)),
            pltpu.SemaphoreType.DMA((HALF,)),
            pltpu.SemaphoreType.DMA((HALF,)),
        ],
        name="add_up",
    )(*parts, so_far)


def shift(value, axis, distance):
    size = math.prod(lax.axis_size(one) for one in (axis if isinstance(axis, tuple) else (axis,)))
    return lax.ppermute(value, axis, [(k, (k + distance) % size) for k in range(size)])


def shift_y(value, distance):
    pairs = []
    for y in range(4):
        to = (y + distance) % 4
        pairs.append((y % 2 * 2 + y // 2, to % 2 * 2 + to // 2))
    return lax.ppermute(value, ("yl", "yh"), pairs)


def tie(*values):
    return lax.optimization_barrier(values)


def per_device(a_vals, a_pos, a_count, b_vals, b_pos, b_count):
    row = lax.axis_index(ROW)
    place = jnp.stack([lax.axis_index("yl"), lax.axis_index("yh"), row, lax.axis_index("z")]).astype(jnp.int32)
    pa, pb = pack(
        a_pos.reshape(SA),
        a_count.reshape(1),
        b_pos.reshape(2, SB),
        b_count.reshape(2),
        a_vals.reshape(SA * BLOCK, BLOCK),
        b_vals.reshape(2 * SB * BLOCK, BLOCK),
    )
    up1, down1, swapped, facing = tie(
        shift(pa, "z", 1), shift(pa, "z", -1), shift(pb, "yl", 1), shift(pb, ROW, 4)
    )
    both = jnp.concatenate([pb, swapped], axis=0)
    up2, down2, high1, low1, other_facing = tie(
        shift(up1, "z", 1),
        shift(down1, "z", -1),
        shift(both, ROW, 1),
        shift(both, ROW, -1),
        shift(facing, "yl", 1),
    )
    density = [pa, up1, down1, up2, down2]
    gram = [both, high1, low1]
    lower = product(False, NEAR, place, density, gram, None, False)
    high2, low2 = shift(high1, ROW, 1), shift(low1, ROW, -1)
    up3, down3, lower = tie(shift(up2, "z", 1), shift(down2, "z", -1), lower)
    gram += [high2, low2]
    size = lax.axis_size("z")
    pairs = [(c * size + k, c * size + (k + 1 - 2 * c) % size) for c in range(2) for k in range(size)]
    opposite = lax.ppermute(jnp.where(lax.axis_index("core") == 0, up3, down3), ("core", "z"), pairs)
    high3, low3 = shift(high2, ROW, 1), shift(low2, ROW, -1)
    lower = product(False, NEXT, place, density, gram, lower, False)
    opposite, high3, low3, lower = tie(opposite, high3, low3, lower)
    density += [up3, down3, opposite]
    gram += [high3, low3, facing, other_facing]

    def exchange(own, q2, qp, qm):
        return own, (shift_y(q2, 2), shift_y(qp, 1), shift_y(qm, -1)), q2

    out, parts1, done = exchange(*product(False, FAR, place, density, gram, lower, True))
    density[0], _ = tie(pa, done)
    out, parts2, _ = exchange(*product(True, NEAR + NEXT + FAR, place, density, gram, None, True, out))
    return add_up(True, parts2, add_up(False, parts1, out))


def solution(mesh):
    cores = 2
    x = mesh.shape["row"] // cores
    z = mesh.shape["col"] // 2
    split = Mesh(mesh.devices.reshape(x, cores, 2, z, mesh.shape["layer"]), ("x", "core", "yl", "z", "yh"))
    lead = (("x", "core"), ("yl", "z"), "yh")
    return jax.shard_map(
        per_device,
        mesh=split,
        in_specs=(P(*lead), P(*lead), P(*lead), P(*lead), P(*lead), P(*lead)),
        out_specs=P(("x", "core"), ("yl", "z", "yh")),
        check_vma=False,
    )
```

```python
import functools
import math

import jax
import jax.numpy as jnp
from jax import lax
from jax.experimental import pallas as pl
from jax.experimental.pallas import tpu as pltpu
from jax.sharding import Mesh
from jax.sharding import PartitionSpec as P

BLOCK = 128
KB = 4
CB = 8
RB = 8
SA = 24
SB = 6
HALF = RB // 2
META = 16
SPARE = 64
ROWS_A = SA * BLOCK + SPARE + META
ROWS_B = SB * BLOCK + META
OFFSETS = (0, -1, 1, -2, 2, -3, 3, 4)
HEIGHT = HALF * BLOCK
ROW = ("x", "core")
NEAR = (0, 1, 2)
NEXT = (3, 4)
FAR = (5, 6, 7)
STEPS = 64.0
TOP = 32760.0
LOWEST = -120.0
MIB = 1024 * 1024

HBM = pl.BlockSpec(memory_space=pltpu.HBM)
ANY = pl.BlockSpec(memory_space=pl.ANY)
SMEM = pl.BlockSpec(memory_space=pltpu.SMEM)
VMEM = pl.BlockSpec(memory_space=pltpu.VMEM)


def pack_kernel(a_pos, a_count, b_pos, b_count, a_vals, b_vals, pa, pb, place):
    lane = lax.broadcasted_iota(jnp.int32, (META, BLOCK), 1)
    for h in range(2):
        start = h * ROWS_B
        pb[start : start + SB * BLOCK, :] = b_vals[h * SB * BLOCK : (h + 1) * SB * BLOCK, :]
        words = jnp.zeros((META, BLOCK), jnp.int32)
        for s in range(SB):
            words = jnp.where(lane == s, b_pos[h, s], words)
        words = jnp.where(lane == SB, b_count[h], words)
        pb[start + SB * BLOCK : start + ROWS_B, :] = words.astype(jnp.float32).astype(jnp.bfloat16)
    pa[...] = jnp.zeros_like(pa)
    for p in range(KB * RB):
        place[p] = -1
    for s in range(SA):
        place[a_pos[s]] = jnp.where(s < a_count[0], s, -1)

    def send(p, carry):
        rank, low, words = carry
        slot = place[p]
        live = slot >= 0
        start = pl.ds(pl.multiple_of(jnp.maximum(slot, 0) * BLOCK, BLOCK), BLOCK)

        @pl.when(live)
        def _():
            pa[pl.ds(pl.multiple_of(rank * BLOCK, BLOCK), BLOCK), :] = a_vals[start, :]

        one = live.astype(jnp.int32)
        words = jnp.where((lane == rank) & live, p, words)
        return rank + one, low + jnp.where(p < HALF * KB, one, 0), words

    words = jnp.zeros((META, BLOCK), jnp.int32)
    total, low, words = lax.fori_loop(0, KB * RB, send, (jnp.int32(0), jnp.int32(0), words))
    words = jnp.where(lane == SA, low, words)
    words = jnp.where(lane == SA + 1, total, words)
    pa[ROWS_A - META :, :] = words.astype(jnp.float32).astype(jnp.bfloat16)


def pack(a_pos, a_count, b_pos, b_count, a_vals, b_vals):
    return pl.pallas_call(
        pack_kernel,
        out_shape=[
            jax.ShapeDtypeStruct((ROWS_A, BLOCK), jnp.bfloat16),
            jax.ShapeDtypeStruct((2 * ROWS_B, BLOCK), jnp.bfloat16),
        ],
        in_specs=[SMEM, SMEM, SMEM, SMEM, VMEM, VMEM],
        out_specs=[VMEM] * 2,
        scratch_shapes=[pltpu.SMEM((KB * RB,), jnp.int32)],
        name="pack",
    )(a_pos, a_count, b_pos, b_count, a_vals, b_vals)


def product_kernel(upper, panels, first, last, place, *refs):
    count = len(panels)
    refs = list(refs)
    density = {p: refs.pop(0) for p in panels}
    gram = {p: [refs.pop(0) for _ in range(1 if p < 7 else 2)] for p in panels}
    so_far = refs.pop(0) if upper else None
    acc_in = None if first else refs.pop(0)
    outs = [refs.pop(0) for _ in range(4 if last else 1)]
    a_buf, b_buf, dense, acc, meta, words, said = refs[:7]
    sem_a, sem_b, sem_am, sem_bm, sem_w = refs[7:]
    yl, yh, i, z = (place[k] for k in range(4))

    def a_copy(n, p):
        return pltpu.make_async_copy(density[p], a_buf.at[n], sem_a.at[n])

    def a_meta(n, p):
        return pltpu.make_async_copy(density[p].at[pl.ds(ROWS_A - META, META)], meta.at[n], sem_am.at[n])

    def gram_rows(p, group, start, rows):
        residue = lax.rem(i + z + OFFSETS[p] + 8, 8)
        stack = jnp.where(residue < i, 1 - yl, yl)
        start = (group * 2 * (2 - len(gram[p])) + stack) * ROWS_B + start
        return gram[p][group % len(gram[p])].at[pl.ds(pl.multiple_of(start, META), rows)]

    def b_meta(n, p, group):
        k = n * 2 + group
        return pltpu.make_async_copy(gram_rows(p, group, SB * BLOCK, META), meta.at[count + k], sem_bm.at[k])

    def b_copy(n, p, group):
        source = gram_rows(p, group, 0, SB * BLOCK)
        return pltpu.make_async_copy(source, b_buf.at[n, group], sem_b.at[n * 2 + group])

    for n, p in enumerate(panels):
        a_meta(n, p).start()
        for group in range(2):
            b_meta(n, p, group).start()
    if not first:
        acc_copy = pltpu.make_async_copy(acc_in, acc, sem_w.at[1])
        acc_copy.start()
    for n, p in enumerate(panels):
        a_copy(n, p).start()
        for group in range(2):
            b_copy(n, p, group).start()

    for n, p in enumerate(panels):
        a_meta(n, p).wait()
        for group in range(2):
            b_meta(n, p, group).wait()
    for k in range(3 * count):
        words[pl.ds(k, 1), :] = meta[k].astype(jnp.float32)[:1].astype(jnp.int32)
    to_scalars = pltpu.make_async_copy(words, said, sem_w.at[0])
    to_scalars.start()
    dense[...] = jnp.zeros_like(dense)
    if first:
        acc[...] = jnp.zeros_like(acc)
    to_scalars.wait()
    if not first:
        acc_copy.wait()

    blank = jnp.zeros((BLOCK, BLOCK), jnp.bfloat16)
    for n, p in enumerate(panels):
        a_copy(n, p).wait()
        for group in range(2):
            b_copy(n, p, group).wait()

        def put(s, carry, n=n):
            at = said[n, s]
            row = lax.shift_right_logical(at, 2) - (HALF if upper else 0)
            to = pl.multiple_of(row * BLOCK, BLOCK)
            start = pl.multiple_of(s * BLOCK, BLOCK)
            dense[n, lax.rem(at, KB), pl.ds(to, BLOCK), :] = a_buf[n, pl.ds(start, BLOCK), :]
            return carry

        low, total = said[n, SA], said[n, SA + 1]
        lax.fori_loop(*((low, total) if upper else (0, low)), put, 0)

        for s in range(SB):
            for group in range(2):
                k = count + 2 * n + group
                at = said[k, s]
                live = s < said[k, SB]
                right = jnp.where(live, b_buf[n, group, s * BLOCK : (s + 1) * BLOCK, :], blank)
                left = dense[n, lax.shift_right_logical(at, 3)]
                acc[group * CB + lax.rem(at, CB)] += jnp.dot(left, right, preferred_element_type=jnp.float32)

    if not last:
        out_copy = pltpu.make_async_copy(acc, outs[0], sem_w.at[2])
        out_copy.start()
        out_copy.wait()
        return
    own_out, q2_out, qp_out, qm_out = outs
    rows = pl.ds(HEIGHT if upper else 0, HEIGHT)
    own_copies = [
        pltpu.make_async_copy(acc.at[yh * (CB // 2) + c], own_out.at[rows, pl.ds(c * BLOCK, BLOCK)], sem_w.at[3 + c])
        for c in range(CB // 2)
    ]
    for copy in own_copies:
        copy.start()
    row = lax.broadcasted_iota(jnp.int32, (META, BLOCK), 0)
    for q_out, group, side in (
        (q2_out, 0, 1 - yh),
        (qp_out, 1, jnp.where(yl == 1, 1 - yh, yh)),
        (qm_out, 1, jnp.where(yl == 1, yh, 1 - yh)),
    ):
        for c in range(CB // 2):
            columns = slice(c * BLOCK, (c + 1) * BLOCK)
            codes = jnp.zeros((META, BLOCK), jnp.float32)
            for r in range(HALF):
                rows = slice(r * BLOCK, (r + 1) * BLOCK)
                value = acc[group * CB + side * (CB // 2) + c, rows, :]
                peak = jnp.max(jnp.max(jnp.abs(value), axis=0, keepdims=True), axis=1, keepdims=True)
                code = jnp.ceil(jnp.maximum(jnp.log2(peak), LOWEST) * STEPS)
                scaled = value * (TOP * jnp.exp2(code * (-1.0 / STEPS)))
                q_out[rows, columns] = jnp.round(scaled).astype(jnp.int32).astype(jnp.int16)
                codes = jnp.where(row == r, code, codes)
            q_out[HEIGHT:, columns] = codes.astype(jnp.int32).astype(jnp.int16)
    for copy in own_copies:
        copy.wait()


def product(upper, panels, place, density, gram, so_far, last, out=None):
    sent = jax.ShapeDtypeStruct((HEIGHT + META, CB // 2 * BLOCK), jnp.int16)
    count = len(panels)
    arrays = [density[p] for p in panels] + [one for p in panels for one in (gram[p : p + 1] if p < 7 else gram[7:9])]
    if upper:
        arrays.append(out)
    first = so_far is None
    if not first:
        arrays.append(so_far)
    if last:
        outs = [jax.ShapeDtypeStruct((RB * BLOCK, CB // 2 * BLOCK), jnp.float32), sent, sent, sent]
    else:
        outs = jax.ShapeDtypeStruct((2 * CB, HEIGHT, BLOCK), jnp.float32)
    return pl.pallas_call(
        functools.partial(product_kernel, upper, panels, first, last),
        out_shape=outs,
        in_specs=[SMEM] + [HBM] * (len(arrays) - (not first)) + [ANY] * (not first),
        out_specs=[HBM, VMEM, VMEM, VMEM] if last else ANY,
        input_output_aliases={len(arrays): 0} if upper else {},
        scratch_shapes=[
            pltpu.VMEM((count, ROWS_A, BLOCK), jnp.bfloat16),
            pltpu.VMEM((count, 2, SB * BLOCK, BLOCK), jnp.bfloat16),
            pltpu.VMEM((count, KB, HEIGHT, BLOCK), jnp.bfloat16),
            pltpu.VMEM((2 * CB, HEIGHT, BLOCK), jnp.float32),
            pltpu.VMEM((3 * count, META, BLOCK), jnp.bfloat16),
            pltpu.VMEM((24, BLOCK), jnp.int32),
            pltpu.SMEM((24, BLOCK), jnp.int32),
            pltpu.SemaphoreType.DMA((count,)),
            pltpu.SemaphoreType.DMA((2 * count,)),
            pltpu.SemaphoreType.DMA((count,)),
            pltpu.SemaphoreType.DMA((2 * count,)),
            pltpu.SemaphoreType.DMA((3 + CB // 2,)),
        ],
        compiler_params=pltpu.CompilerParams(vmem_limit_bytes=(8 + 2 * count) * MIB),
        cost_estimate=pl.CostEstimate(flops=1_000_000_000 * count, bytes_accessed=2_000_000 * count, transcendentals=0),
        name=("upper" if upper else "lower") + str(count) + ("_last" if last else ""),
    )(place, *arrays)


def sum_kernel(skip, *refs):
    parts, so_far, out, own, sem_in, sem_out = refs[:3], *refs[3:]

    def read(r):
        rows = pl.ds(r * BLOCK, BLOCK)
        return pltpu.make_async_copy(so_far.at[pl.ds((skip + r) * BLOCK, BLOCK)], own.at[rows], sem_in.at[r])

    def write(r):
        rows = pl.ds(r * BLOCK, BLOCK)
        return pltpu.make_async_copy(own.at[rows], out.at[pl.ds((skip + r) * BLOCK, BLOCK)], sem_out.at[r])

    for r in range(HALF):
        read(r).start()
    scales = []
    for k in range(3):
        codes = parts[k][HEIGHT:, :].astype(jnp.int32).astype(jnp.float32)
        scales.append(jnp.exp2(codes * (1.0 / STEPS)) * (1.0 / TOP))
    for r in range(HALF):
        rows = pl.ds(r * BLOCK, BLOCK)
        read(r).wait()
        value = own[rows, :]
        for k in range(3):
            value = value + parts[k][rows, :].astype(jnp.int32).astype(jnp.float32) * scales[k][r : r + 1]
        own[rows, :] = value
        write(r).start()
    for r in range(HALF):
        write(r).wait()


def add_up(upper, parts, so_far):
    width = CB // 2 * BLOCK
    return pl.pallas_call(
        functools.partial(sum_kernel, HALF if upper else 0),
        out_shape=jax.ShapeDtypeStruct((RB * BLOCK, width), jnp.float32),
        in_specs=[VMEM] * 3 + [HBM],
        out_specs=HBM,
        input_output_aliases={3: 0},
        scratch_shapes=[
            pltpu.VMEM((HEIGHT, width), jnp.float32),
            pltpu.SemaphoreType.DMA((HALF,)),
            pltpu.SemaphoreType.DMA((HALF,)),
        ],
        compiler_params=pltpu.CompilerParams(vmem_limit_bytes=6 * MIB),
        name="add_up",
    )(*parts, so_far)


def shift(value, axis, distance):
    size = math.prod(lax.axis_size(one) for one in (axis if isinstance(axis, tuple) else (axis,)))
    return lax.ppermute(value, axis, [(k, (k + distance) % size) for k in range(size)])


def shift_y(value, distance):
    pairs = []
    for y in range(4):
        to = (y + distance) % 4
        pairs.append((y % 2 * 2 + y // 2, to % 2 * 2 + to // 2))
    return lax.ppermute(value, ("yl", "yh"), pairs)


def tie(*values):
    return lax.optimization_barrier(values)


def per_device(a_vals, a_pos, a_count, b_vals, b_pos, b_count):
    row = lax.axis_index(ROW)
    place = jnp.stack([lax.axis_index("yl"), lax.axis_index("yh"), row, lax.axis_index("z")]).astype(jnp.int32)
    pa, pb = pack(
        a_pos.reshape(SA),
        a_count.reshape(1),
        b_pos.reshape(2, SB),
        b_count.reshape(2),
        a_vals.reshape(SA * BLOCK, BLOCK),
        b_vals.reshape(2 * SB * BLOCK, BLOCK),
    )
    up1, down1, facing = tie(shift(pa, "z", 1), shift(pa, "z", -1), shift(pb, ROW, 4))
    both = jnp.concatenate([pb, shift(pb, "yl", 1)], axis=0)
    high1, low1 = shift(both, ROW, 1), shift(both, ROW, -1)
    up2, down2, other_facing = tie(shift(up1, "z", 1), shift(down1, "z", -1), shift(facing, "yl", 1))
    density = [pa, up1, down1, up2, down2]
    gram = [both, high1, low1]
    lower = product(False, NEAR, place, density, gram, None, False)
    high2, low2 = shift(high1, ROW, 1), shift(low1, ROW, -1)
    up3, down3, lower = tie(shift(up2, "z", 1), shift(down2, "z", -1), lower)
    gram += [high2, low2]
    size = lax.axis_size("z")
    pairs = [(c * size + k, c * size + (k + 1 - 2 * c) % size) for c in range(2) for k in range(size)]
    opposite = lax.ppermute(jnp.where(lax.axis_index("core") == 0, up3, down3), ("core", "z"), pairs)
    high3, low3 = shift(high2, ROW, 1), shift(low2, ROW, -1)
    lower = product(False, NEXT, place, density, gram, lower, False)
    opposite, lower = tie(opposite, lower)
    density += [up3, down3, opposite]
    gram += [high3, low3, facing, other_facing]

    def exchange(own, q2, qp, qm):
        return own, (shift_y(q2, 2), shift_y(qp, 1), shift_y(qm, -1)), q2

    out, parts1, done = exchange(*product(False, FAR, place, density, gram, lower, True))
    density[0], _ = tie(pa, done)
    out, parts2, _ = exchange(*product(True, NEAR + NEXT + FAR, place, density, gram, None, True, out))
    return add_up(True, parts2, add_up(False, parts1, out))


def solution(mesh):
    cores = 2
    x = mesh.shape["row"] // cores
    z = mesh.shape["col"] // 2
    split = Mesh(mesh.devices.reshape(x, cores, 2, z, mesh.shape["layer"]), ("x", "core", "yl", "z", "yh"))
    lead = (("x", "core"), ("yl", "z"), "yh")
    return jax.shard_map(
        per_device,
        mesh=split,
        in_specs=(P(*lead), P(*lead), P(*lead), P(*lead), P(*lead), P(*lead)),
        out_specs=P(("x", "core"), ("yl", "z", "yh")),
        check_vma=False,
    )
```

```python
import functools
import math

import jax
import jax.numpy as jnp
from jax import lax
from jax.experimental import pallas as pl
from jax.experimental.pallas import tpu as pltpu
from jax.sharding import Mesh
from jax.sharding import PartitionSpec as P

BLOCK = 128
KB = 4
CB = 8
RB = 8
SA = 24
SB = 6
HALF = RB // 2
META = 16
SPARE = 64
ROWS_A = SA * BLOCK + SPARE + META
ROWS_B = SB * BLOCK + META
OFFSETS = (0, -1, 1, -2, 2, -3, 3, 4)
HEIGHT = HALF * BLOCK
ROW = ("x", "core")
NEAR = (0, 1, 2)
NEXT = (3, 4)
LATE = (5, 6)
FAR = (7,)
STEPS = 64.0
TOP = 32760.0
LOWEST = -120.0
MIB = 1024 * 1024

HBM = pl.BlockSpec(memory_space=pltpu.HBM)
ANY = pl.BlockSpec(memory_space=pl.ANY)
SMEM = pl.BlockSpec(memory_space=pltpu.SMEM)
VMEM = pl.BlockSpec(memory_space=pltpu.VMEM)


def pack_kernel(a_pos, a_count, b_pos, b_count, a_vals, b_vals, pa, pb, place):
    lane = lax.broadcasted_iota(jnp.int32, (META, BLOCK), 1)
    for h in range(2):
        start = h * ROWS_B
        pb[start : start + SB * BLOCK, :] = b_vals[h * SB * BLOCK : (h + 1) * SB * BLOCK, :]
        words = jnp.zeros((META, BLOCK), jnp.int32)
        for s in range(SB):
            words = jnp.where(lane == s, b_pos[h, s], words)
        words = jnp.where(lane == SB, b_count[h], words)
        pb[start + SB * BLOCK : start + ROWS_B, :] = words.astype(jnp.float32).astype(jnp.bfloat16)
    pa[...] = jnp.zeros_like(pa)
    for p in range(KB * RB):
        place[p] = -1
    for s in range(SA):
        place[a_pos[s]] = jnp.where(s < a_count[0], s, -1)

    def send(p, carry):
        rank, low, words = carry
        slot = place[p]
        live = slot >= 0
        start = pl.ds(pl.multiple_of(jnp.maximum(slot, 0) * BLOCK, BLOCK), BLOCK)

        @pl.when(live)
        def _():
            pa[pl.ds(pl.multiple_of(rank * BLOCK, BLOCK), BLOCK), :] = a_vals[start, :]

        one = live.astype(jnp.int32)
        words = jnp.where((lane == rank) & live, p, words)
        return rank + one, low + jnp.where(p < HALF * KB, one, 0), words

    words = jnp.zeros((META, BLOCK), jnp.int32)
    total, low, words = lax.fori_loop(0, KB * RB, send, (jnp.int32(0), jnp.int32(0), words))
    words = jnp.where(lane == SA, low, words)
    words = jnp.where(lane == SA + 1, total, words)
    pa[ROWS_A - META :, :] = words.astype(jnp.float32).astype(jnp.bfloat16)


def pack(a_pos, a_count, b_pos, b_count, a_vals, b_vals):
    return pl.pallas_call(
        pack_kernel,
        out_shape=[
            jax.ShapeDtypeStruct((ROWS_A, BLOCK), jnp.bfloat16),
            jax.ShapeDtypeStruct((2 * ROWS_B, BLOCK), jnp.bfloat16),
        ],
        in_specs=[SMEM, SMEM, SMEM, SMEM, VMEM, VMEM],
        out_specs=[VMEM] * 2,
        scratch_shapes=[pltpu.SMEM((KB * RB,), jnp.int32)],
        name="pack",
    )(a_pos, a_count, b_pos, b_count, a_vals, b_vals)


def product_kernel(upper, panels, first, last, place, *refs):
    count = len(panels)
    refs = list(refs)
    density = {p: refs.pop(0) for p in panels}
    gram = {p: [refs.pop(0) for _ in range(1 if p < 7 else 2)] for p in panels}
    so_far = refs.pop(0) if upper else None
    acc_in = None if first else refs.pop(0)
    outs = [refs.pop(0) for _ in range(4 if last else 1)]
    a_buf, b_buf, dense, acc, meta, words, said = refs[:7]
    sem_a, sem_b, sem_am, sem_bm, sem_w = refs[7:]
    yl, yh, i, z = (place[k] for k in range(4))

    def a_copy(n, p):
        return pltpu.make_async_copy(density[p], a_buf.at[n], sem_a.at[n])

    def a_meta(n, p):
        return pltpu.make_async_copy(density[p].at[pl.ds(ROWS_A - META, META)], meta.at[n], sem_am.at[n])

    def gram_rows(p, group, start, rows):
        residue = lax.rem(i + z + OFFSETS[p] + 8, 8)
        stack = jnp.where(residue < i, 1 - yl, yl)
        start = (group * 2 * (2 - len(gram[p])) + stack) * ROWS_B + start
        return gram[p][group % len(gram[p])].at[pl.ds(pl.multiple_of(start, META), rows)]

    def b_meta(n, p, group):
        k = n * 2 + group
        return pltpu.make_async_copy(gram_rows(p, group, SB * BLOCK, META), meta.at[count + k], sem_bm.at[k])

    def b_copy(n, p, group):
        source = gram_rows(p, group, 0, SB * BLOCK)
        return pltpu.make_async_copy(source, b_buf.at[n, group], sem_b.at[n * 2 + group])

    for n, p in enumerate(panels):
        a_meta(n, p).start()
        for group in range(2):
            b_meta(n, p, group).start()
    if not first:
        acc_copy = pltpu.make_async_copy(acc_in, acc, sem_w.at[1])
        acc_copy.start()
    for n, p in enumerate(panels):
        a_copy(n, p).start()
        for group in range(2):
            b_copy(n, p, group).start()

    for n, p in enumerate(panels):
        a_meta(n, p).wait()
        for group in range(2):
            b_meta(n, p, group).wait()
    for k in range(3 * count):
        words[pl.ds(k, 1), :] = meta[k].astype(jnp.float32)[:1].astype(jnp.int32)
    to_scalars = pltpu.make_async_copy(words, said, sem_w.at[0])
    to_scalars.start()
    dense[...] = jnp.zeros_like(dense)
    if first:
        acc[...] = jnp.zeros_like(acc)
    to_scalars.wait()
    if not first:
        acc_copy.wait()

    blank = jnp.zeros((BLOCK, BLOCK), jnp.bfloat16)
    for n, p in enumerate(panels):
        a_copy(n, p).wait()
        for group in range(2):
            b_copy(n, p, group).wait()

        def put(s, carry, n=n):
            at = said[n, s]
            row = lax.shift_right_logical(at, 2) - (HALF if upper else 0)
            to = pl.multiple_of(row * BLOCK, BLOCK)
            start = pl.multiple_of(s * BLOCK, BLOCK)
            dense[n, lax.rem(at, KB), pl.ds(to, BLOCK), :] = a_buf[n, pl.ds(start, BLOCK), :]
            return carry

        low, total = said[n, SA], said[n, SA + 1]
        lax.fori_loop(*((low, total) if upper else (0, low)), put, 0)

        for s in range(SB):
            for group in range(2):
                k = count + 2 * n + group
                at = said[k, s]
                live = s < said[k, SB]
                right = jnp.where(live, b_buf[n, group, s * BLOCK : (s + 1) * BLOCK, :], blank)
                left = dense[n, lax.shift_right_logical(at, 3)]
                acc[group * CB + lax.rem(at, CB)] += jnp.dot(left, right, preferred_element_type=jnp.float32)

    if not last:
        out_copy = pltpu.make_async_copy(acc, outs[0], sem_w.at[2])
        out_copy.start()
        out_copy.wait()
        return
    own_out, q2_out, qp_out, qm_out = outs
    rows = pl.ds(HEIGHT if upper else 0, HEIGHT)
    own_copies = [
        pltpu.make_async_copy(acc.at[yh * (CB // 2) + c], own_out.at[rows, pl.ds(c * BLOCK, BLOCK)], sem_w.at[3 + c])
        for c in range(CB // 2)
    ]
    for copy in own_copies:
        copy.start()
    row = lax.broadcasted_iota(jnp.int32, (META, BLOCK), 0)
    for q_out, group, side in (
        (q2_out, 0, 1 - yh),
        (qp_out, 1, jnp.where(yl == 1, 1 - yh, yh)),
        (qm_out, 1, jnp.where(yl == 1, yh, 1 - yh)),
    ):
        for c in range(CB // 2):
            columns = slice(c * BLOCK, (c + 1) * BLOCK)
            codes = jnp.zeros((META, BLOCK), jnp.float32)
            for r in range(HALF):
                rows = slice(r * BLOCK, (r + 1) * BLOCK)
                value = acc[group * CB + side * (CB // 2) + c, rows, :]
                peak = jnp.max(jnp.max(jnp.abs(value), axis=0, keepdims=True), axis=1, keepdims=True)
                code = jnp.ceil(jnp.maximum(jnp.log2(peak), LOWEST) * STEPS)
                scaled = value * (TOP * jnp.exp2(code * (-1.0 / STEPS)))
                q_out[rows, columns] = jnp.round(scaled).astype(jnp.int32).astype(jnp.int16)
                codes = jnp.where(row == r, code, codes)
            q_out[HEIGHT:, columns] = codes.astype(jnp.int32).astype(jnp.int16)
    for copy in own_copies:
        copy.wait()


def product(upper, panels, place, density, gram, so_far, last, out=None):
    sent = jax.ShapeDtypeStruct((HEIGHT + META, CB // 2 * BLOCK), jnp.int16)
    count = len(panels)
    arrays = [density[p] for p in panels] + [one for p in panels for one in (gram[p : p + 1] if p < 7 else gram[7:9])]
    if upper:
        arrays.append(out)
    first = so_far is None
    if not first:
        arrays.append(so_far)
    if last:
        outs = [jax.ShapeDtypeStruct((RB * BLOCK, CB // 2 * BLOCK), jnp.float32), sent, sent, sent]
    else:
        outs = jax.ShapeDtypeStruct((2 * CB, HEIGHT, BLOCK), jnp.float32)
    return pl.pallas_call(
        functools.partial(product_kernel, upper, panels, first, last),
        out_shape=outs,
        in_specs=[SMEM] + [HBM] * (len(arrays) - (not first)) + [ANY] * (not first),
        out_specs=[HBM, VMEM, VMEM, VMEM] if last else ANY,
        input_output_aliases={len(arrays): 0} if upper else {},
        scratch_shapes=[
            pltpu.VMEM((count, ROWS_A, BLOCK), jnp.bfloat16),
            pltpu.VMEM((count, 2, SB * BLOCK, BLOCK), jnp.bfloat16),
            pltpu.VMEM((count, KB, HEIGHT, BLOCK), jnp.bfloat16),
            pltpu.VMEM((2 * CB, HEIGHT, BLOCK), jnp.float32),
            pltpu.VMEM((3 * count, META, BLOCK), jnp.bfloat16),
            pltpu.VMEM((24, BLOCK), jnp.int32),
            pltpu.SMEM((24, BLOCK), jnp.int32),
            pltpu.SemaphoreType.DMA((count,)),
            pltpu.SemaphoreType.DMA((2 * count,)),
            pltpu.SemaphoreType.DMA((count,)),
            pltpu.SemaphoreType.DMA((2 * count,)),
            pltpu.SemaphoreType.DMA((3 + CB // 2,)),
        ],
        compiler_params=pltpu.CompilerParams(vmem_limit_bytes=(8 + 2 * count) * MIB),
        cost_estimate=pl.CostEstimate(flops=1_000_000_000 * count, bytes_accessed=2_000_000 * count, transcendentals=0),
        name=("upper" if upper else "lower") + str(count) + ("_last" if last else ""),
    )(place, *arrays)


def sum_kernel(skip, *refs):
    parts, so_far, out, own, sem_in, sem_out = refs[:3], *refs[3:]

    def read(r):
        rows = pl.ds(r * BLOCK, BLOCK)
        return pltpu.make_async_copy(so_far.at[pl.ds((skip + r) * BLOCK, BLOCK)], own.at[rows], sem_in.at[r])

    def write(r):
        rows = pl.ds(r * BLOCK, BLOCK)
        return pltpu.make_async_copy(own.at[rows], out.at[pl.ds((skip + r) * BLOCK, BLOCK)], sem_out.at[r])

    for r in range(HALF):
        read(r).start()
    scales = []
    for k in range(3):
        codes = parts[k][HEIGHT:, :].astype(jnp.int32).astype(jnp.float32)
        scales.append(jnp.exp2(codes * (1.0 / STEPS)) * (1.0 / TOP))
    for r in range(HALF):
        rows = pl.ds(r * BLOCK, BLOCK)
        read(r).wait()
        value = own[rows, :]
        for k in range(3):
            value = value + parts[k][rows, :].astype(jnp.int32).astype(jnp.float32) * scales[k][r : r + 1]
        own[rows, :] = value
        write(r).start()
    for r in range(HALF):
        write(r).wait()


def add_up(upper, parts, so_far):
    width = CB // 2 * BLOCK
    return pl.pallas_call(
        functools.partial(sum_kernel, HALF if upper else 0),
        out_shape=jax.ShapeDtypeStruct((RB * BLOCK, width), jnp.float32),
        in_specs=[VMEM] * 3 + [HBM],
        out_specs=HBM,
        input_output_aliases={3: 0},
        scratch_shapes=[
            pltpu.VMEM((HEIGHT, width), jnp.float32),
            pltpu.SemaphoreType.DMA((HALF,)),
            pltpu.SemaphoreType.DMA((HALF,)),
        ],
        compiler_params=pltpu.CompilerParams(vmem_limit_bytes=6 * MIB),
        name="add_up",
    )(*parts, so_far)


def shift(value, axis, distance):
    size = math.prod(lax.axis_size(one) for one in (axis if isinstance(axis, tuple) else (axis,)))
    return lax.ppermute(value, axis, [(k, (k + distance) % size) for k in range(size)])


def shift_y(value, distance):
    pairs = []
    for y in range(4):
        to = (y + distance) % 4
        pairs.append((y % 2 * 2 + y // 2, to % 2 * 2 + to // 2))
    return lax.ppermute(value, ("yl", "yh"), pairs)


def tie(*values):
    return lax.optimization_barrier(values)


def per_device(a_vals, a_pos, a_count, b_vals, b_pos, b_count):
    row = lax.axis_index(ROW)
    place = jnp.stack([lax.axis_index("yl"), lax.axis_index("yh"), row, lax.axis_index("z")]).astype(jnp.int32)
    pa, pb = pack(
        a_pos.reshape(SA),
        a_count.reshape(1),
        b_pos.reshape(2, SB),
        b_count.reshape(2),
        a_vals.reshape(SA * BLOCK, BLOCK),
        b_vals.reshape(2 * SB * BLOCK, BLOCK),
    )
    up1, down1, facing = tie(shift(pa, "z", 1), shift(pa, "z", -1), shift(pb, ROW, 4))
    both = jnp.concatenate([pb, shift(pb, "yl", 1)], axis=0)
    high1, low1 = shift(both, ROW, 1), shift(both, ROW, -1)
    up2, down2, other_facing = tie(shift(up1, "z", 1), shift(down1, "z", -1), shift(facing, "yl", 1))
    density = [pa, up1, down1, up2, down2]
    gram = [both, high1, low1]
    lower = product(False, NEAR, place, density, gram, None, False)
    high2, low2 = shift(high1, ROW, 1), shift(low1, ROW, -1)
    up3, down3, lower = tie(shift(up2, "z", 1), shift(down2, "z", -1), lower)
    gram += [high2, low2]
    size = lax.axis_size("z")
    pairs = [(c * size + k, c * size + (k + 1 - 2 * c) % size) for c in range(2) for k in range(size)]
    opposite = lax.ppermute(jnp.where(lax.axis_index("core") == 0, up3, down3), ("core", "z"), pairs)
    high3, low3 = shift(high2, ROW, 1), shift(low2, ROW, -1)
    lower = product(False, NEXT, place, density, gram, lower, False)
    density += [up3, down3]
    gram += [high3, low3]
    lower = product(False, LATE, place, density, gram, lower, False)
    opposite, lower = tie(opposite, lower)
    density.append(opposite)
    gram += [facing, other_facing]

    def exchange(own, q2, qp, qm):
        return own, (shift_y(q2, 2), shift_y(qp, 1), shift_y(qm, -1)), q2

    out, parts1, done = exchange(*product(False, FAR, place, density, gram, lower, True))
    density[0], _ = tie(pa, done)
    out, parts2, _ = exchange(*product(True, NEAR + NEXT + LATE + FAR, place, density, gram, None, True, out))
    return add_up(True, parts2, add_up(False, parts1, out))


def solution(mesh):
    cores = 2
    x = mesh.shape["row"] // cores
    z = mesh.shape["col"] // 2
    split = Mesh(mesh.devices.reshape(x, cores, 2, z, mesh.shape["layer"]), ("x", "core", "yl", "z", "yh"))
    lead = (("x", "core"), ("yl", "z"), "yh")
    return jax.shard_map(
        per_device,
        mesh=split,
        in_specs=(P(*lead), P(*lead), P(*lead), P(*lead), P(*lead), P(*lead)),
        out_specs=P(("x", "core"), ("yl", "z", "yh")),
        check_vma=False,
    )
```

```python
import functools
import math

import jax
import jax.numpy as jnp
from jax import lax
from jax.experimental import pallas as pl
from jax.experimental.pallas import tpu as pltpu
from jax.sharding import Mesh
from jax.sharding import PartitionSpec as P

BLOCK = 128
KB = 4
CB = 8
RB = 8
SA = 24
SB = 6
HALF = RB // 2
META = 16
SPARE = 64
ROWS_A = SA * BLOCK + SPARE + META
ROWS_B = SB * BLOCK + META
OFFSETS = (0, -1, 1, -2, 2, -3, 3, 4)
HEIGHT = HALF * BLOCK
ROW = ("x", "core")
OWN = (0,)
NEAR = (1, 2)
NEXT = (3, 4)
LATE = (5, 6)
FAR = (7,)
STEPS = 64.0
TOP = 32760.0
LOWEST = -120.0
MIB = 1024 * 1024

HBM = pl.BlockSpec(memory_space=pltpu.HBM)
ANY = pl.BlockSpec(memory_space=pl.ANY)
SMEM = pl.BlockSpec(memory_space=pltpu.SMEM)
VMEM = pl.BlockSpec(memory_space=pltpu.VMEM)


def pack_kernel(a_pos, a_count, b_pos, b_count, a_vals, b_vals, pa, pb, place):
    lane = lax.broadcasted_iota(jnp.int32, (META, BLOCK), 1)
    for h in range(2):
        start = h * ROWS_B
        pb[start : start + SB * BLOCK, :] = b_vals[h * SB * BLOCK : (h + 1) * SB * BLOCK, :]
        words = jnp.zeros((META, BLOCK), jnp.int32)
        for s in range(SB):
            words = jnp.where(lane == s, b_pos[h, s], words)
        words = jnp.where(lane == SB, b_count[h], words)
        pb[start + SB * BLOCK : start + ROWS_B, :] = words.astype(jnp.float32).astype(jnp.bfloat16)
    pa[...] = jnp.zeros_like(pa)
    for p in range(KB * RB):
        place[p] = -1
    for s in range(SA):
        place[a_pos[s]] = jnp.where(s < a_count[0], s, -1)

    def send(p, carry):
        rank, low, words = carry
        slot = place[p]
        live = slot >= 0
        start = pl.ds(pl.multiple_of(jnp.maximum(slot, 0) * BLOCK, BLOCK), BLOCK)

        @pl.when(live)
        def _():
            pa[pl.ds(pl.multiple_of(rank * BLOCK, BLOCK), BLOCK), :] = a_vals[start, :]

        one = live.astype(jnp.int32)
        words = jnp.where((lane == rank) & live, p, words)
        return rank + one, low + jnp.where(p < HALF * KB, one, 0), words

    words = jnp.zeros((META, BLOCK), jnp.int32)
    total, low, words = lax.fori_loop(0, KB * RB, send, (jnp.int32(0), jnp.int32(0), words))
    words = jnp.where(lane == SA, low, words)
    words = jnp.where(lane == SA + 1, total, words)
    pa[ROWS_A - META :, :] = words.astype(jnp.float32).astype(jnp.bfloat16)


def pack(a_pos, a_count, b_pos, b_count, a_vals, b_vals):
    return pl.pallas_call(
        pack_kernel,
        out_shape=[
            jax.ShapeDtypeStruct((ROWS_A, BLOCK), jnp.bfloat16),
            jax.ShapeDtypeStruct((2 * ROWS_B, BLOCK), jnp.bfloat16),
        ],
        in_specs=[SMEM, SMEM, SMEM, SMEM, VMEM, VMEM],
        out_specs=[VMEM] * 2,
        scratch_shapes=[pltpu.SMEM((KB * RB,), jnp.int32)],
        name="pack",
    )(a_pos, a_count, b_pos, b_count, a_vals, b_vals)


def product_kernel(upper, panels, first, last, place, *refs):
    count = len(panels)
    refs = list(refs)
    density = {p: refs.pop(0) for p in panels}
    gram = {p: [refs.pop(0) for _ in range(1 if p < 7 else 2)] for p in panels}
    so_far = refs.pop(0) if upper else None
    acc_in = None if first else refs.pop(0)
    outs = [refs.pop(0) for _ in range(4 if last else 1)]
    a_buf, b_buf, dense, acc, meta, words, said = refs[:7]
    sem_a, sem_b, sem_am, sem_bm, sem_w = refs[7:]
    yl, yh, i, z = (place[k] for k in range(4))

    def a_copy(n, p):
        return pltpu.make_async_copy(density[p], a_buf.at[n], sem_a.at[n])

    def a_meta(n, p):
        return pltpu.make_async_copy(density[p].at[pl.ds(ROWS_A - META, META)], meta.at[n], sem_am.at[n])

    def gram_rows(p, group, start, rows):
        residue = lax.rem(i + z + OFFSETS[p] + 8, 8)
        stack = jnp.where(residue < i, 1 - yl, yl)
        start = (group * 2 * (2 - len(gram[p])) + stack) * ROWS_B + start
        return gram[p][group % len(gram[p])].at[pl.ds(pl.multiple_of(start, META), rows)]

    def b_meta(n, p, group):
        k = n * 2 + group
        return pltpu.make_async_copy(gram_rows(p, group, SB * BLOCK, META), meta.at[count + k], sem_bm.at[k])

    def b_copy(n, p, group):
        source = gram_rows(p, group, 0, SB * BLOCK)
        return pltpu.make_async_copy(source, b_buf.at[n, group], sem_b.at[n * 2 + group])

    for n, p in enumerate(panels):
        a_meta(n, p).start()
        for group in range(2):
            b_meta(n, p, group).start()
    if not first:
        acc_copy = pltpu.make_async_copy(acc_in, acc, sem_w.at[1])
        acc_copy.start()
    for n, p in enumerate(panels):
        a_copy(n, p).start()
        for group in range(2):
            b_copy(n, p, group).start()

    for n, p in enumerate(panels):
        a_meta(n, p).wait()
        for group in range(2):
            b_meta(n, p, group).wait()
    for k in range(3 * count):
        words[pl.ds(k, 1), :] = meta[k].astype(jnp.float32)[:1].astype(jnp.int32)
    to_scalars = pltpu.make_async_copy(words, said, sem_w.at[0])
    to_scalars.start()
    dense[...] = jnp.zeros_like(dense)
    if first:
        acc[...] = jnp.zeros_like(acc)
    to_scalars.wait()
    if not first:
        acc_copy.wait()

    blank = jnp.zeros((BLOCK, BLOCK), jnp.bfloat16)
    for n, p in enumerate(panels):
        a_copy(n, p).wait()
        for group in range(2):
            b_copy(n, p, group).wait()

        def put(s, carry, n=n):
            at = said[n, s]
            row = lax.shift_right_logical(at, 2) - (HALF if upper else 0)
            to = pl.multiple_of(row * BLOCK, BLOCK)
            start = pl.multiple_of(s * BLOCK, BLOCK)
            dense[n, lax.rem(at, KB), pl.ds(to, BLOCK), :] = a_buf[n, pl.ds(start, BLOCK), :]
            return carry

        low, total = said[n, SA], said[n, SA + 1]
        lax.fori_loop(*((low, total) if upper else (0, low)), put, 0)

        for s in range(SB):
            for group in range(2):
                k = count + 2 * n + group
                at = said[k, s]
                live = s < said[k, SB]
                right = jnp.where(live, b_buf[n, group, s * BLOCK : (s + 1) * BLOCK, :], blank)
                left = dense[n, lax.shift_right_logical(at, 3)]
                acc[group * CB + lax.rem(at, CB)] += jnp.dot(left, right, preferred_element_type=jnp.float32)

    if not last:
        out_copy = pltpu.make_async_copy(acc, outs[0], sem_w.at[2])
        out_copy.start()
        out_copy.wait()
        return
    own_out, q2_out, qp_out, qm_out = outs
    rows = pl.ds(HEIGHT if upper else 0, HEIGHT)
    own_copies = [
        pltpu.make_async_copy(acc.at[yh * (CB // 2) + c], own_out.at[rows, pl.ds(c * BLOCK, BLOCK)], sem_w.at[3 + c])
        for c in range(CB // 2)
    ]
    for copy in own_copies:
        copy.start()
    row = lax.broadcasted_iota(jnp.int32, (META, BLOCK), 0)
    for q_out, group, side in (
        (q2_out, 0, 1 - yh),
        (qp_out, 1, jnp.where(yl == 1, 1 - yh, yh)),
        (qm_out, 1, jnp.where(yl == 1, yh, 1 - yh)),
    ):
        for c in range(CB // 2):
            columns = slice(c * BLOCK, (c + 1) * BLOCK)
            codes = jnp.zeros((META, BLOCK), jnp.float32)
            for r in range(HALF):
                rows = slice(r * BLOCK, (r + 1) * BLOCK)
                value = acc[group * CB + side * (CB // 2) + c, rows, :]
                peak = jnp.max(jnp.max(jnp.abs(value), axis=0, keepdims=True), axis=1, keepdims=True)
                code = jnp.ceil(jnp.maximum(jnp.log2(peak), LOWEST) * STEPS)
                scaled = value * (TOP * jnp.exp2(code * (-1.0 / STEPS)))
                q_out[rows, columns] = jnp.round(scaled).astype(jnp.int32).astype(jnp.int16)
                codes = jnp.where(row == r, code, codes)
            q_out[HEIGHT:, columns] = codes.astype(jnp.int32).astype(jnp.int16)
    for copy in own_copies:
        copy.wait()


def product(upper, panels, place, density, gram, so_far, last, out=None):
    sent = jax.ShapeDtypeStruct((HEIGHT + META, CB // 2 * BLOCK), jnp.int16)
    count = len(panels)
    arrays = [density[p] for p in panels] + [one for p in panels for one in (gram[p : p + 1] if p < 7 else gram[7:9])]
    if upper:
        arrays.append(out)
    first = so_far is None
    if not first:
        arrays.append(so_far)
    if last:
        outs = [jax.ShapeDtypeStruct((RB * BLOCK, CB // 2 * BLOCK), jnp.float32), sent, sent, sent]
    else:
        outs = jax.ShapeDtypeStruct((2 * CB, HEIGHT, BLOCK), jnp.float32)
    return pl.pallas_call(
        functools.partial(product_kernel, upper, panels, first, last),
        out_shape=outs,
        in_specs=[SMEM] + [HBM] * (len(arrays) - (not first)) + [ANY] * (not first),
        out_specs=[HBM, VMEM, VMEM, VMEM] if last else ANY,
        input_output_aliases={len(arrays): 0} if upper else {},
        scratch_shapes=[
            pltpu.VMEM((count, ROWS_A, BLOCK), jnp.bfloat16),
            pltpu.VMEM((count, 2, SB * BLOCK, BLOCK), jnp.bfloat16),
            pltpu.VMEM((count, KB, HEIGHT, BLOCK), jnp.bfloat16),
            pltpu.VMEM((2 * CB, HEIGHT, BLOCK), jnp.float32),
            pltpu.VMEM((3 * count, META, BLOCK), jnp.bfloat16),
            pltpu.VMEM((24, BLOCK), jnp.int32),
            pltpu.SMEM((24, BLOCK), jnp.int32),
            pltpu.SemaphoreType.DMA((count,)),
            pltpu.SemaphoreType.DMA((2 * count,)),
            pltpu.SemaphoreType.DMA((count,)),
            pltpu.SemaphoreType.DMA((2 * count,)),
            pltpu.SemaphoreType.DMA((3 + CB // 2,)),
        ],
        compiler_params=pltpu.CompilerParams(vmem_limit_bytes=(8 + 2 * count) * MIB),
        cost_estimate=pl.CostEstimate(flops=1_000_000_000 * count, bytes_accessed=2_000_000 * count, transcendentals=0),
        name=("upper" if upper else "lower") + str(count) + ("_last" if last else ""),
    )(place, *arrays)


def sum_kernel(skip, *refs):
    parts, so_far, out, own, sem_in, sem_out = refs[:3], *refs[3:]

    def read(r):
        rows = pl.ds(r * BLOCK, BLOCK)
        return pltpu.make_async_copy(so_far.at[pl.ds((skip + r) * BLOCK, BLOCK)], own.at[rows], sem_in.at[r])

    def write(r):
        rows = pl.ds(r * BLOCK, BLOCK)
        return pltpu.make_async_copy(own.at[rows], out.at[pl.ds((skip + r) * BLOCK, BLOCK)], sem_out.at[r])

    for r in range(HALF):
        read(r).start()
    scales = []
    for k in range(3):
        codes = parts[k][HEIGHT:, :].astype(jnp.int32).astype(jnp.float32)
        scales.append(jnp.exp2(codes * (1.0 / STEPS)) * (1.0 / TOP))
    for r in range(HALF):
        rows = pl.ds(r * BLOCK, BLOCK)
        read(r).wait()
        value = own[rows, :]
        for k in range(3):
            value = value + parts[k][rows, :].astype(jnp.int32).astype(jnp.float32) * scales[k][r : r + 1]
        own[rows, :] = value
        write(r).start()
    for r in range(HALF):
        write(r).wait()


def add_up(upper, parts, so_far):
    width = CB // 2 * BLOCK
    return pl.pallas_call(
        functools.partial(sum_kernel, HALF if upper else 0),
        out_shape=jax.ShapeDtypeStruct((RB * BLOCK, width), jnp.float32),
        in_specs=[VMEM] * 3 + [HBM],
        out_specs=HBM,
        input_output_aliases={3: 0},
        scratch_shapes=[
            pltpu.VMEM((HEIGHT, width), jnp.float32),
            pltpu.SemaphoreType.DMA((HALF,)),
            pltpu.SemaphoreType.DMA((HALF,)),
        ],
        compiler_params=pltpu.CompilerParams(vmem_limit_bytes=6 * MIB),
        name="add_up",
    )(*parts, so_far)


def shift(value, axis, distance):
    size = math.prod(lax.axis_size(one) for one in (axis if isinstance(axis, tuple) else (axis,)))
    return lax.ppermute(value, axis, [(k, (k + distance) % size) for k in range(size)])


def shift_y(value, distance):
    pairs = []
    for y in range(4):
        to = (y + distance) % 4
        pairs.append((y % 2 * 2 + y // 2, to % 2 * 2 + to // 2))
    return lax.ppermute(value, ("yl", "yh"), pairs)


def tie(*values):
    return lax.optimization_barrier(values)


def per_device(a_vals, a_pos, a_count, b_vals, b_pos, b_count):
    row = lax.axis_index(ROW)
    place = jnp.stack([lax.axis_index("yl"), lax.axis_index("yh"), row, lax.axis_index("z")]).astype(jnp.int32)
    pa, pb = pack(
        a_pos.reshape(SA),
        a_count.reshape(1),
        b_pos.reshape(2, SB),
        b_count.reshape(2),
        a_vals.reshape(SA * BLOCK, BLOCK),
        b_vals.reshape(2 * SB * BLOCK, BLOCK),
    )
    up1, down1, facing = tie(shift(pa, "z", 1), shift(pa, "z", -1), shift(pb, ROW, 4))
    both = jnp.concatenate([pb, shift(pb, "yl", 1)], axis=0)
    high1, low1 = shift(both, ROW, 1), shift(both, ROW, -1)
    lower = product(False, OWN, place, [pa], [both], None, False)
    up2, down2, other_facing, lower = tie(
        shift(up1, "z", 1), shift(down1, "z", -1), shift(facing, "yl", 1), lower
    )
    density = [pa, up1, down1, up2, down2]
    gram = [both, high1, low1]
    lower = product(False, NEAR, place, density, gram, lower, False)
    high2, low2 = shift(high1, ROW, 1), shift(low1, ROW, -1)
    up3, down3, lower = tie(shift(up2, "z", 1), shift(down2, "z", -1), lower)
    gram += [high2, low2]
    size = lax.axis_size("z")
    pairs = [(c * size + k, c * size + (k + 1 - 2 * c) % size) for c in range(2) for k in range(size)]
    opposite = lax.ppermute(jnp.where(lax.axis_index("core") == 0, up3, down3), ("core", "z"), pairs)
    high3, low3 = shift(high2, ROW, 1), shift(low2, ROW, -1)
    lower = product(False, NEXT, place, density, gram, lower, False)
    density += [up3, down3]
    gram += [high3, low3]
    lower = product(False, LATE, place, density, gram, lower, False)
    opposite, lower = tie(opposite, lower)
    density.append(opposite)
    gram += [facing, other_facing]

    def exchange(own, q2, qp, qm):
        return own, (shift_y(q2, 2), shift_y(qp, 1), shift_y(qm, -1)), q2

    out, parts1, done = exchange(*product(False, FAR, place, density, gram, lower, True))
    density[0], _ = tie(pa, done)
    out, parts2, _ = exchange(*product(True, OWN + NEAR + NEXT + LATE + FAR, place, density, gram, None, True, out))
    return add_up(True, parts2, add_up(False, parts1, out))


def solution(mesh):
    cores = 2
    x = mesh.shape["row"] // cores
    z = mesh.shape["col"] // 2
    split = Mesh(mesh.devices.reshape(x, cores, 2, z, mesh.shape["layer"]), ("x", "core", "yl", "z", "yh"))
    lead = (("x", "core"), ("yl", "z"), "yh")
    return jax.shard_map(
        per_device,
        mesh=split,
        in_specs=(P(*lead), P(*lead), P(*lead), P(*lead), P(*lead), P(*lead)),
        out_specs=P(("x", "core"), ("yl", "z", "yh")),
        check_vma=False,
    )
```
